32 devices in a mesh: groups: 2 (over y), vec: 4 (over z), space: 4 (over x, core).
Axes of the slice: x: 2, y: 2, z: 4, core: 2. Of those that a mesh axis runs over, the one named last changes fastest.
Arguments:
- left_vecs: bfloat16 [1024, 4, 3, 4, 2304], P('vec', 'groups', None, 'space'), parts along dimension 1, may hold values from -6 to 6
- right_vecs: bfloat16 [128, 4, 3, 4, 2304], P('vec', 'groups', None, 'space'), parts along dimension 1, may hold values from -6 to 6
- gauge_links: float32 [6, 2, 3, 3, 4, 2304], P('groups', None, None, None, 'space'), parts along dimension 0, may hold values from -2.5 to 2.5
- momenta: int32 [16, 3], replicated, may hold values from -2 to 2
- column_order: int32 [128], replicated, may hold values from 0 to 127, each once
Outputs:
- mesons: float32 [16, 4, 1024, 128], P('space', 'groups', 'vec'), parts along dimension 1
The draws below stay inside these ranges and needn't reach their ends.
There are 2 independent parts, one for each index of `groups`. The reference program is written for one: setup_inputs(seed, part) draws one part's arguments, and reference() takes and returns one part's arrays. A program takes and returns all parts, laid end to end along the dimension named above; an argument that names none is the same for every part. Nothing has to cross between parts.
Inputs may be any that keep to these rules, and one draw needn't show every extreme that they name: `momenta`: each momentum component lies in -2 to 2. `column_order`: a permutation of the right vectors.
All inputs are finite; a program needn't handle non-finite values.
Results may differ from the reference program's by a relative error of at most 0.0039.
Values may be sent and summed in bfloat16 or wider, within the bound.
A program may use at most 192 MiB of HBM per device.

```python
import math
import jax
import jax.numpy as jnp
from jax import lax

NL = 1024
NR = 128
NP = 16
LY = 48
LZ = 48
NX = 4
YZ = 2304


def plant(entries, stream_key, least, largest):
    longest = entries.shape.index(max(entries.shape))
    spots = []
    for shift in (0, 1):
        where = [jax.random.randint(jax.random.fold_in(stream_key, axis), (), 0, length) for axis, length in enumerate(entries.shape)]
        where[longest] = (where[longest] + shift) % entries.shape[longest]
        spots.append(tuple(where))
    return entries.at[spots[0]].set(least).at[spots[1]].set(largest)


def shard_levels(own_key, dims, pieces, low, high):
    gain = 1.0
    for axis_at, shards_of in pieces:
        draws = jax.random.uniform(jax.random.fold_in(jax.random.fold_in(own_key, 6), axis_at), (shards_of,), jnp.float32, low / len(pieces), high / len(pieces))
        gain = gain * jnp.repeat(jnp.exp(draws), dims[axis_at] // shards_of).reshape((-1,) + (1,) * (len(dims) - 1 - axis_at))
    return gain


def centred(own_key, dims, spread, most, split=(), kind=jnp.bfloat16):
    drawn = jax.random.normal(own_key, dims, jnp.float32) * spread
    if len(split) > 0:
        drawn = shard_levels(own_key, dims, split, -0.22, 0.18) * drawn
    return jnp.clip(drawn, min=-most, max=most).astype(kind)


def setup_inputs(seed: int = 0, part: int = 0) -> dict:
    key_of = jax.random.split(jax.random.key(seed), 6)
    part_keys = jax.random.split(jax.random.fold_in(key_of[5], part), 6)
    left_vecs = centred(part_keys[0], (NL, 2, 3, NX, YZ), 1.0, 6.0, ((0, 4), (3, 4)))
    right_vecs = centred(part_keys[1], (NR, 2, 3, NX, YZ), 1.0, 6.0, ((0, 4), (3, 4)))
    gauge_links = centred(part_keys[2], (3, 2, 3, 3, NX, YZ), 0.35, 2.5, ((4, 4),), jnp.float32)
    momenta = plant(jax.random.randint(key_of[3], (NP, 3), -2, 3), jax.random.fold_in(key_of[3], 1), -2, 2).astype(jnp.int32)
    column_order = jax.random.permutation(key_of[4], NR).astype(jnp.int32)
    return dict(left_vecs=left_vecs, right_vecs=right_vecs, gauge_links=gauge_links, momenta=momenta, column_order=column_order)


def shifted(field, direction, step, width_z):
    length = field.shape[-1]
    if direction == 1:
        return jnp.roll(field, -step * width_z, axis=-1)
    column = jnp.arange(length) % width_z
    if step == 1:
        return jnp.where(column == width_z - 1, jnp.roll(field, width_z - 1, axis=-1), jnp.roll(field, -1, axis=-1))
    return jnp.where(column == 0, jnp.roll(field, 1 - width_z, axis=-1), jnp.roll(field, 1, axis=-1))

def color_mul(matrix, vectors):
    return lax.optimization_barrier(jnp.sum(matrix[None] * vectors[:, None], axis=2))

def link_apply(link, vectors, adjoint):
    real_part = link[0]
    imag_part = link[1]
    if adjoint:
        real_part = jnp.swapaxes(real_part, 0, 1)
        imag_part = -jnp.swapaxes(imag_part, 0, 1)
    vec_real = vectors[:, 0]
    vec_imag = vectors[:, 1]
    out_real = color_mul(real_part, vec_real) - color_mul(imag_part, vec_imag)
    out_imag = color_mul(real_part, vec_imag) + color_mul(imag_part, vec_real)
    return jnp.stack([out_real, out_imag], axis=1)

def laplace_hops(center, plus_x, minus_x, links, back_x, width_z):
    total = link_apply(links[0], plus_x, False) + link_apply(back_x, minus_x, True)
    for direction in (1, 2):
        total = total + link_apply(links[direction], shifted(center, direction, 1, width_z), False)
        total = total + link_apply(shifted(links[direction], direction, -1, width_z), shifted(center, direction, -1, width_z), True)
    return total - 6.0 * center

def phase_tables(momenta, global_x, count_x, width_y, width_z, length):
    sites = jnp.arange(length)
    coord_y = sites // width_z
    coord_z = sites % width_z
    two_pi = 2.0 * math.pi
    angle_x = jnp.mod(momenta[:, 0:1] * global_x[None], count_x).astype(jnp.float32) * (two_pi / count_x)
    angle_y = jnp.mod(momenta[:, 1:2] * coord_y[None], width_y).astype(jnp.float32) * (two_pi / width_y)
    angle_z = jnp.mod(momenta[:, 2:3] * coord_z[None], width_z).astype(jnp.float32) * (two_pi / width_z)
    angle = angle_x[:, :, None] + (angle_y + angle_z)[:, None, :]
    return (jnp.cos(angle), jnp.sin(angle))

def fold_phase(vectors, cosine, sine):
    values = vectors.astype(jnp.float32)
    vec_real = values[:, 0]
    vec_imag = values[:, 1]
    real_out = vec_real * cosine - vec_imag * sine
    imag_out = -(vec_real * sine + vec_imag * cosine)
    folded = jnp.stack([real_out, imag_out], axis=1).astype(jnp.bfloat16)
    return folded.reshape(folded.shape[0], 2, -1)

def combine_parts(product):
    return jnp.stack([product[..., 0, :, 0] - product[..., 1, :, 1], product[..., 0, :, 1] + product[..., 1, :, 0]], axis=-3)

def reference(left_vecs, right_vecs, gauge_links, momenta, column_order):
    fields = right_vecs.astype(jnp.float32)
    smeared = laplace_hops(fields, jnp.roll(fields, -1, axis=3), jnp.roll(fields, 1, axis=3), gauge_links, jnp.roll(gauge_links[0], 1, axis=3), LZ).astype(jnp.bfloat16)
    stacked = smeared.astype(jnp.float32).reshape(NR, 2, -1)
    cosine, sine = phase_tables(momenta, jnp.arange(NX), NX, LY, LZ, LY * LZ)

    def one_momentum(index):
        folded = fold_phase(left_vecs, cosine[index], sine[index]).astype(jnp.float32)
        product = lax.dot_general(folded, stacked, (((2,), (2,)), ((), ())), precision=lax.Precision.HIGHEST)
        return combine_parts(product)
    mesons = lax.map(one_momentum, jnp.arange(NP))
    mesons = mesons * (1.0 / (8.0 * math.sqrt(3.0 * NX * LY * LZ)))
    return jnp.take(mesons, column_order, axis=3)
```

```python
import math

import jax
import jax.numpy as jnp
from jax import lax
from jax.experimental import pallas as pl
from jax.experimental.pallas import tpu as pltpu
from jax.sharding import PartitionSpec as P

LZ = 48


def with_halo(block, sides, width):
    for axis, dim in sides:
        count = lax.axis_size(axis)
        forward = [(i, i + 1) for i in range(count - 1)]
        forward.append((count - 1, 0))
        backward = [(target, source) for source, target in forward]
        low = lax.ppermute(
            lax.slice_in_dim(block, block.shape[dim] - width, None, axis=dim), axis, forward
        )
        high = lax.ppermute(lax.slice_in_dim(block, 0, width, axis=dim), axis, backward)
        block = jnp.concatenate([low, block, high], axis=dim)
    return block


def from_behind(array, axis, by):
    length = lax.axis_size(axis)
    return lax.ppermute(array, axis, [(i, (i + by) % length) for i in range(length)])


def shifted(field, direction, step, width_z):
    length = field.shape[-1]
    if direction == 1:
        return jnp.roll(field, -step * width_z, axis=-1)
    column = jnp.arange(length) % width_z
    if step == 1:
        return jnp.where(
            column == width_z - 1,
            jnp.roll(field, width_z - 1, axis=-1),
            jnp.roll(field, -1, axis=-1),
        )
    return jnp.where(
        column == 0, jnp.roll(field, 1 - width_z, axis=-1), jnp.roll(field, 1, axis=-1)
    )


def color_mul(matrix, vectors):
    return jnp.sum(matrix[None] * vectors[:, None], axis=2)


def link_apply(link, vectors, adjoint):
    real_part = link[0]
    imag_part = link[1]
    if adjoint:
        real_part = jnp.swapaxes(real_part, 0, 1)
        imag_part = -jnp.swapaxes(imag_part, 0, 1)
    vec_real = vectors[:, 0]
    vec_imag = vectors[:, 1]
    out_real = color_mul(real_part, vec_real) - color_mul(imag_part, vec_imag)
    out_imag = color_mul(real_part, vec_imag) + color_mul(imag_part, vec_real)
    return jnp.stack([out_real, out_imag], axis=1)


def laplace_hops(center, plus_x, minus_x, links, back_x, width_z):
    total = link_apply(links[0], plus_x, False) + link_apply(back_x, minus_x, True)
    for direction in (1, 2):
        total = total + link_apply(links[direction], shifted(center, direction, 1, width_z), False)
        total = total + link_apply(
            shifted(links[direction], direction, -1, width_z),
            shifted(center, direction, -1, width_z),
            True,
        )
    return total - 6.0 * center


def phase_tables(momenta, global_x, count_x, width_y, width_z, length):
    sites = jnp.arange(length)
    coord_y = sites // width_z
    coord_z = sites % width_z
    two_pi = 2.0 * math.pi
    angle_x = jnp.mod(momenta[:, 0:1] * global_x[None], count_x).astype(jnp.float32) * (
        two_pi / count_x
    )
    angle_y = jnp.mod(momenta[:, 1:2] * coord_y[None], width_y).astype(jnp.float32) * (
        two_pi / width_y
    )
    angle_z = jnp.mod(momenta[:, 2:3] * coord_z[None], width_z).astype(jnp.float32) * (
        two_pi / width_z
    )
    angle = angle_x[:, :, None] + (angle_y + angle_z)[:, None, :]
    return (jnp.cos(angle), jnp.sin(angle))


def fold_phase(vectors, cosine, sine):
    values = vectors.astype(jnp.float32)
    vec_real = values[:, 0]
    vec_imag = values[:, 1]
    real_out = vec_real * cosine - vec_imag * sine
    imag_out = -(vec_real * sine + vec_imag * cosine)
    folded = jnp.stack([real_out, imag_out], axis=1).astype(jnp.bfloat16)
    return folded.reshape(folded.shape[0], 2, -1)


def combine_parts(product):
    return jnp.stack(
        [
            product[..., 0, :, 0] - product[..., 1, :, 1],
            product[..., 0, :, 1] + product[..., 1, :, 0],
        ],
        axis=-3,
    )


def contract(folded, stacked):
    product = lax.dot_general(
        folded, stacked, (((folded.ndim - 1,), (2,)), ((), ())), preferred_element_type=jnp.float32
    )
    return combine_parts(product)


def local_plain(left_vecs, right_vecs, gauge_links, momenta, column_order):
    local_x = left_vecs.shape[3]
    plane_size = left_vecs.shape[4]
    space_count = lax.axis_size("space")
    total_x = local_x * space_count
    padded = with_halo(right_vecs, (("space", 3),), 1)
    last_plane = gauge_links[0, :, :, :, local_x - 1 :, :]
    previous = from_behind(last_plane, "space", 1)
    back_x = jnp.concatenate([previous, gauge_links[0, :, :, :, : local_x - 1, :]], axis=3)
    global_x = lax.axis_index("space") * local_x + jnp.arange(local_x)
    cosine, sine = phase_tables(momenta, global_x, total_x, plane_size // LZ, LZ, plane_size)
    folded_all = jax.vmap(fold_phase, in_axes=(None, 0, 0))(left_vecs, cosine, sine)
    fields = padded.astype(jnp.float32)
    center = fields[:, :, :, 1:-1, :]
    smeared = laplace_hops(
        center, fields[:, :, :, 2:, :], fields[:, :, :, :-2, :], gauge_links, back_x, LZ
    ).astype(jnp.bfloat16)
    piece = lax.all_gather(smeared, "vec", axis=0, tiled=True)
    stacked = piece.reshape(piece.shape[0], 2, -1)
    mesons = contract(folded_all, stacked)
    hot = (jnp.arange(column_order.shape[0])[:, None] == column_order[None]).astype(jnp.float32)
    mesons = jnp.einsum("prij,jk->prik", mesons, hot, precision=lax.Precision.HIGHEST)
    scale = 1.0 / (8.0 * math.sqrt(3.0 * total_x * plane_size))
    share = lax.psum_scatter(mesons, "space", scatter_dimension=0, tiled=True)
    return share * scale


ROWS = 16
TILE = 256
PIECE = 768


def fast_kernel(
    v_ref, plus_ref, minus_ref, link_ref, back_ref, cos_ref, sin_ref, hot_ref, l_ref, out_ref,
    hops, moved, gath, both, acc, outbox, own, inbox, total,
    gsend, grecv, rsend, rrecv,
):
    nvec = lax.axis_size("vec")
    nspace = lax.axis_size("space")
    vec = lax.axis_index("vec")
    space = lax.axis_index("space")
    sites = v_ref.shape[2]
    chunks = v_ref.shape[1] // ROWS
    momenta = cos_ref.shape[0]
    share = momenta // nspace
    slots = nvec * chunks
    left = l_ref.shape[0]

    barrier = pltpu.get_barrier_semaphore()
    for k in range(1, nvec):
        pl.semaphore_signal(barrier, inc=1, device_id={"vec": lax.rem(vec + k, nvec)},
                            device_id_type=pl.DeviceIdType.MESH)
    for k in range(1, nspace):
        pl.semaphore_signal(barrier, inc=1, device_id={"space": lax.rem(space + k, nspace)},
                            device_id_type=pl.DeviceIdType.MESH)

    column = lax.rem(lax.broadcasted_iota(jnp.int32, (1, sites), 1), LZ)

    def roll(x, by):
        return pltpu.roll(x, by % sites, 1)

    def z_up(x):
        return jnp.where(column == LZ - 1, roll(x, LZ - 1), roll(x, -1))

    def z_down(x):
        return jnp.where(column == 0, roll(x, 1 - LZ), roll(x, 1))

    hops[0] = link_ref[0]
    hops[1] = back_ref[...]
    hops[2] = link_ref[1]
    hops[3] = roll(link_ref[1], LZ)
    hops[4] = link_ref[2]
    hops[5] = z_down(link_ref[2])

    pl.semaphore_wait(barrier, nvec - 1 + nspace - 1)

    def gather_copy(c, k):
        slot = vec * chunks + c
        return pltpu.make_async_remote_copy(
            src_ref=gath.at[slot], dst_ref=gath.at[slot],
            send_sem=gsend.at[c, k - 1], recv_sem=grecv.at[c, k - 1],
            device_id={"vec": lax.rem(vec + k, nvec)}, device_id_type=pl.DeviceIdType.MESH)

    def smear(c, carry):
        rows = pl.ds(pl.multiple_of(c * ROWS, ROWS), ROWS)

        def shift(comp, carry):
            x = v_ref[comp, rows, :].astype(jnp.float32)
            moved[0, comp] = plus_ref[comp, rows, :].astype(jnp.float32)
            moved[1, comp] = minus_ref[comp, rows, :].astype(jnp.float32)
            moved[2, comp] = roll(x, -LZ)
            moved[3, comp] = roll(x, LZ)
            moved[4, comp] = z_up(x)
            moved[5, comp] = z_down(x)
            return carry

        lax.fori_loop(0, 6, shift, 0)
        slot = vec * chunks + c

        def lanes(t, carry):
            at = pl.multiple_of(t * TILE, TILE)
            cols = pl.ds(at, TILE)
            re = [-6.0 * v_ref[2 * a, rows, cols].astype(jnp.float32) for a in range(3)]
            im = [-6.0 * v_ref[2 * a + 1, rows, cols].astype(jnp.float32) for a in range(3)]
            for h in range(6):
                for b in range(3):
                    vr = moved[h, 2 * b, :, cols]
                    vi = moved[h, 2 * b + 1, :, cols]
                    for a in range(3):
                        row = 3 * a + b if h % 2 == 0 else 3 * b + a
                        ur = hops[h, row : row + 1, cols]
                        ui = hops[h, 9 + row : 10 + row, cols]
                        if h % 2 == 0:
                            re[a] = re[a] + (ur * vr - ui * vi)
                            im[a] = im[a] + (ur * vi + ui * vr)
                        else:
                            re[a] = re[a] + (ur * vr + ui * vi)
                            im[a] = im[a] + (ur * vi - ui * vr)
            for a in range(3):
                base = 2 * a * sites
                gath[slot, :, pl.ds(pl.multiple_of(at + base, TILE), TILE)] = re[a].astype(jnp.bfloat16)
                gath[slot, :, pl.ds(pl.multiple_of(at + base + sites, TILE), TILE)] = im[a].astype(jnp.bfloat16)
            return carry

        lax.fori_loop(0, sites // TILE, lanes, 0)
        for k in range(1, nvec):
            gather_copy(c, k).start()
        return carry

    lax.fori_loop(0, chunks, smear, 0)

    def reduce_copy(t, k):
        to = lax.rem(space + k, nspace)
        return pltpu.make_async_remote_copy(
            src_ref=outbox.at[t, to], dst_ref=inbox.at[t, k - 1],
            send_sem=rsend.at[t, k - 1], recv_sem=rrecv.at[t, k - 1],
            device_id={"space": to}, device_id_type=pl.DeviceIdType.MESH)

    def owner_slot(t):
        u = t - chunks
        far = u % (nvec - 1)
        k = jnp.where(t < chunks, 0, 1 + (2 * far) % (nvec - 1))
        c = jnp.where(t < chunks, t, u // (nvec - 1))
        return k, c, lax.rem(vec - k + nvec, nvec) * chunks + c

    block = momenta * ROWS

    def step(t, carry):
        k, c, slot = owner_slot(t)

        @pl.when(t >= chunks)
        def _():
            pltpu.make_async_remote_copy(
                src_ref=gath.at[slot], dst_ref=gath.at[slot],
                send_sem=gsend.at[c, k - 1], recv_sem=grecv.at[c, k - 1],
                device_id={"vec": lax.rem(vec + k, nvec)},
                device_id_type=pl.DeviceIdType.MESH).wait_recv()

        acc[...] = jnp.zeros_like(acc)
        parts = sites // PIECE

        def piece(q, carry):
            colour = q // parts
            tile = q % parts
            at = pl.multiple_of(tile * PIECE, PIECE)
            real_at = pl.multiple_of(colour * 2 * sites + tile * PIECE, PIECE)
            imag_at = pl.multiple_of(real_at + sites, PIECE)
            sr = gath[slot, :, pl.ds(real_at, PIECE)].astype(jnp.float32)
            si = gath[slot, :, pl.ds(imag_at, PIECE)].astype(jnp.float32)
            for p in range(momenta):
                cs = cos_ref[p : p + 1, pl.ds(at, PIECE)]
                sn = sin_ref[p : p + 1, pl.ds(at, PIECE)]
                both[p * ROWS : (p + 1) * ROWS, :] = (sr * cs + si * sn).astype(jnp.bfloat16)
                both[block + p * ROWS : block + (p + 1) * ROWS, :] = (si * cs - sr * sn).astype(jnp.bfloat16)
            dims = (((1,), (1,)), ((), ()))
            d1 = lax.dot_general(both[...], l_ref[:, pl.ds(real_at, PIECE)], dims,
                                 preferred_element_type=jnp.float32)
            d2 = lax.dot_general(both[...], l_ref[:, pl.ds(imag_at, PIECE)], dims,
                                 preferred_element_type=jnp.float32)
            acc[0] += d1[:block] + d2[block:]
            acc[1] += d1[block:] - d2[:block]
            return carry

        lax.fori_loop(0, 3 * parts, piece, 0)
        mine = share * ROWS
        for d in range(nspace):
            outbox[t, d] = acc[:, d * mine : (d + 1) * mine, :].astype(jnp.bfloat16)
        own[t] = acc[:, pl.ds(pl.multiple_of(space * mine, mine), mine), :]
        for m in range(1, nspace):
            reduce_copy(t, m).start()
        return carry

    lax.fori_loop(0, slots, step, 0)

    def finish(t, carry):
        k, c, slot = owner_slot(t)
        for m in range(1, nspace):
            reduce_copy(t, m).wait()
        value = own[t]
        for m in range(1, nspace):
            value = value + inbox[t, m - 1].astype(jnp.float32)
        at = pl.ds(pl.multiple_of(slot * ROWS, ROWS), ROWS)
        for r in range(2):
            for p in range(share):
                total[r, p, at, :] = value[r, p * ROWS : (p + 1) * ROWS, :]
        return carry

    lax.fori_loop(0, slots, finish, 0)
    scale = 1.0 / (8.0 * math.sqrt(3.0 * nspace * sites))
    hot = hot_ref[...]
    dims = (((0,), (0,)), ((), ()))
    for r in range(2):
        for p in range(share):
            x = total[r, p] * scale
            high = x.astype(jnp.bfloat16)
            low = (x - high.astype(jnp.float32)).astype(jnp.bfloat16)
            out_ref[p, r] = lax.dot_general(
                high, hot, dims, preferred_element_type=jnp.float32
            ) + lax.dot_general(low, hot, dims, preferred_element_type=jnp.float32)
    for c in range(chunks):
        for k in range(1, nvec):
            gather_copy(c, k).wait_send()


def local_fast(left_vecs, right_vecs, gauge_links, momenta, column_order):
    left = left_vecs.shape[0]
    right = right_vecs.shape[0]
    sites = left_vecs.shape[4]
    nspace = lax.axis_size("space")
    nvec = lax.axis_size("vec")
    count = momenta.shape[0]
    share = count // nspace
    chunks = right // ROWS
    slots = nvec * chunks
    center = right_vecs.transpose(2, 1, 3, 0, 4).reshape(6, right, sites)
    plus = from_behind(center, "space", -1)
    minus = from_behind(center, "space", 1)
    links = gauge_links.reshape(3, 18, sites)
    back = from_behind(links[0], "space", 1)
    rows = left_vecs.transpose(0, 2, 1, 3, 4).reshape(left, 6 * sites)
    cosine, sine = phase_tables(
        momenta, lax.axis_index("space")[None], nspace, sites // LZ, LZ, sites
    )
    cosine, sine = cosine.reshape(count, sites), sine.reshape(count, sites)
    hot = (jnp.arange(nvec * right)[:, None] == column_order[None]).astype(jnp.bfloat16)
    vmem = pl.BlockSpec(memory_space=pltpu.VMEM)
    mine = share * ROWS
    return pl.pallas_call(
        fast_kernel,
        out_shape=jax.ShapeDtypeStruct((share, 2, left, nvec * right), jnp.float32),
        in_specs=[vmem] * 9,
        out_specs=vmem,
        scratch_shapes=[
            pltpu.VMEM((6, 18, sites), jnp.float32),
            pltpu.VMEM((6, 6, ROWS, sites), jnp.float32),
            pltpu.VMEM((slots, ROWS, 6 * sites), jnp.bfloat16),
            pltpu.VMEM((2 * count * ROWS, PIECE), jnp.bfloat16),
            pltpu.VMEM((2, count * ROWS, left), jnp.float32),
            pltpu.VMEM((slots, nspace, 2, mine, left), jnp.bfloat16),
            pltpu.VMEM((slots, 2, mine, left), jnp.float32),
            pltpu.VMEM((slots, nspace - 1, 2, mine, left), jnp.bfloat16),
            pltpu.VMEM((2, share, nvec * right, left), jnp.float32),
            pltpu.SemaphoreType.DMA((chunks, nvec - 1)),
            pltpu.SemaphoreType.DMA((chunks, nvec - 1)),
            pltpu.SemaphoreType.DMA((slots, nspace - 1)),
            pltpu.SemaphoreType.DMA((slots, nspace - 1)),
        ],
        compiler_params=pltpu.CompilerParams(
            collective_id=0, has_side_effects=True, vmem_limit_bytes=56 * 1024 * 1024
        ),
        cost_estimate=pl.CostEstimate(flops=30_000_000_000, bytes_accessed=20_000_000, transcendentals=0),
    )(center, plus, minus, links, back, cosine, sine, hot, rows)


def local(left_vecs, right_vecs, gauge_links, momenta, column_order):
    nvec = lax.axis_size("vec")
    nspace = lax.axis_size("space")
    fits = (
        left_vecs.shape[3] == 1
        and right_vecs.shape[0] % ROWS == 0
        and nvec == 4
        and nspace == 4
        and left_vecs.shape[4] % PIECE == 0
        and momenta.shape[0] % nspace == 0
    )
    chosen = local_fast if fits else local_plain
    return chosen(left_vecs, right_vecs, gauge_links, momenta, column_order)


def solution(mesh):
    in_specs = (
        P("vec", "groups", None, "space", None),
        P("vec", "groups", None, "space", None),
        P("groups", None, None, None, "space", None),
        P(),
        P(),
    )
    out_specs = P("space", "groups", "vec", None)
    return jax.shard_map(local, mesh=mesh, in_specs=in_specs, out_specs=out_specs, check_vma=False)
```

```python
import math

import jax
import jax.numpy as jnp
from jax import lax
from jax.experimental import pallas as pl
from jax.experimental.pallas import tpu as pltpu
from jax.sharding import PartitionSpec as P

LZ = 48


def with_halo(block, sides, width):
    for axis, dim in sides:
        count = lax.axis_size(axis)
        forward = [(i, i + 1) for i in range(count - 1)]
        forward.append((count - 1, 0))
        backward = [(target, source) for source, target in forward]
        low = lax.ppermute(
            lax.slice_in_dim(block, block.shape[dim] - width, None, axis=dim), axis, forward
        )
        high = lax.ppermute(lax.slice_in_dim(block, 0, width, axis=dim), axis, backward)
        block = jnp.concatenate([low, block, high], axis=dim)
    return block


def from_behind(array, axis, by):
    length = lax.axis_size(axis)
    return lax.ppermute(array, axis, [(i, (i + by) % length) for i in range(length)])


def shifted(field, direction, step, width_z):
    length = field.shape[-1]
    if direction == 1:
        return jnp.roll(field, -step * width_z, axis=-1)
    column = jnp.arange(length) % width_z
    if step == 1:
        return jnp.where(
            column == width_z - 1,
            jnp.roll(field, width_z - 1, axis=-1),
            jnp.roll(field, -1, axis=-1),
        )
    return jnp.where(
        column == 0, jnp.roll(field, 1 - width_z, axis=-1), jnp.roll(field, 1, axis=-1)
    )


def color_mul(matrix, vectors):
    return jnp.sum(matrix[None] * vectors[:, None], axis=2)


def link_apply(link, vectors, adjoint):
    real_part = link[0]
    imag_part = link[1]
    if adjoint:
        real_part = jnp.swapaxes(real_part, 0, 1)
        imag_part = -jnp.swapaxes(imag_part, 0, 1)
    vec_real = vectors[:, 0]
    vec_imag = vectors[:, 1]
    out_real = color_mul(real_part, vec_real) - color_mul(imag_part, vec_imag)
    out_imag = color_mul(real_part, vec_imag) + color_mul(imag_part, vec_real)
    return jnp.stack([out_real, out_imag], axis=1)


def laplace_hops(center, plus_x, minus_x, links, back_x, width_z):
    total = link_apply(links[0], plus_x, False) + link_apply(back_x, minus_x, True)
    for direction in (1, 2):
        total = total + link_apply(links[direction], shifted(center, direction, 1, width_z), False)
        total = total + link_apply(
            shifted(links[direction], direction, -1, width_z),
            shifted(center, direction, -1, width_z),
            True,
        )
    return total - 6.0 * center


def phase_tables(momenta, global_x, count_x, width_y, width_z, length):
    sites = jnp.arange(length)
    coord_y = sites // width_z
    coord_z = sites % width_z
    two_pi = 2.0 * math.pi
    angle_x = jnp.mod(momenta[:, 0:1] * global_x[None], count_x).astype(jnp.float32) * (
        two_pi / count_x
    )
    angle_y = jnp.mod(momenta[:, 1:2] * coord_y[None], width_y).astype(jnp.float32) * (
        two_pi / width_y
    )
    angle_z = jnp.mod(momenta[:, 2:3] * coord_z[None], width_z).astype(jnp.float32) * (
        two_pi / width_z
    )
    angle = angle_x[:, :, None] + (angle_y + angle_z)[:, None, :]
    return (jnp.cos(angle), jnp.sin(angle))


def fold_phase(vectors, cosine, sine):
    values = vectors.astype(jnp.float32)
    vec_real = values[:, 0]
    vec_imag = values[:, 1]
    real_out = vec_real * cosine - vec_imag * sine
    imag_out = -(vec_real * sine + vec_imag * cosine)
    folded = jnp.stack([real_out, imag_out], axis=1).astype(jnp.bfloat16)
    return folded.reshape(folded.shape[0], 2, -1)


def combine_parts(product):
    return jnp.stack(
        [
            product[..., 0, :, 0] - product[..., 1, :, 1],
            product[..., 0, :, 1] + product[..., 1, :, 0],
        ],
        axis=-3,
    )


def contract(folded, stacked):
    product = lax.dot_general(
        folded, stacked, (((folded.ndim - 1,), (2,)), ((), ())), preferred_element_type=jnp.float32
    )
    return combine_parts(product)


def local_plain(left_vecs, right_vecs, gauge_links, momenta, column_order):
    local_x = left_vecs.shape[3]
    plane_size = left_vecs.shape[4]
    space_count = lax.axis_size("space")
    total_x = local_x * space_count
    padded = with_halo(right_vecs, (("space", 3),), 1)
    last_plane = gauge_links[0, :, :, :, local_x - 1 :, :]
    previous = from_behind(last_plane, "space", 1)
    back_x = jnp.concatenate([previous, gauge_links[0, :, :, :, : local_x - 1, :]], axis=3)
    global_x = lax.axis_index("space") * local_x + jnp.arange(local_x)
    cosine, sine = phase_tables(momenta, global_x, total_x, plane_size // LZ, LZ, plane_size)
    folded_all = jax.vmap(fold_phase, in_axes=(None, 0, 0))(left_vecs, cosine, sine)
    fields = padded.astype(jnp.float32)
    center = fields[:, :, :, 1:-1, :]
    smeared = laplace_hops(
        center, fields[:, :, :, 2:, :], fields[:, :, :, :-2, :], gauge_links, back_x, LZ
    ).astype(jnp.bfloat16)
    piece = lax.all_gather(smeared, "vec", axis=0, tiled=True)
    stacked = piece.reshape(piece.shape[0], 2, -1)
    mesons = contract(folded_all, stacked)
    hot = (jnp.arange(column_order.shape[0])[:, None] == column_order[None]).astype(jnp.float32)
    mesons = jnp.einsum("prij,jk->prik", mesons, hot, precision=lax.Precision.HIGHEST)
    scale = 1.0 / (8.0 * math.sqrt(3.0 * total_x * plane_size))
    share = lax.psum_scatter(mesons, "space", scatter_dimension=0, tiled=True)
    return share * scale


ROWS = 16
TILE = 256
PIECE = 768


def fast_kernel(
    v_ref, plus_ref, minus_ref, link_ref, back_ref, cos_ref, sin_ref, hot_ref, l_ref, out_ref,
    hops, moved, gath, both, acc, outbox, own, inbox, total,
    gsend, grecv, rsend, rrecv,
):
    nvec = lax.axis_size("vec")
    nspace = lax.axis_size("space")
    vec = lax.axis_index("vec")
    space = lax.axis_index("space")
    sites = v_ref.shape[2]
    chunks = v_ref.shape[1] // ROWS
    momenta = cos_ref.shape[0]
    share = momenta // nspace
    slots = nvec * chunks
    left = l_ref.shape[0]

    barrier = pltpu.get_barrier_semaphore()
    for k in range(1, nvec):
        pl.semaphore_signal(barrier, inc=1, device_id={"vec": lax.rem(vec + k, nvec)},
                            device_id_type=pl.DeviceIdType.MESH)
    for k in range(1, nspace):
        pl.semaphore_signal(barrier, inc=1, device_id={"space": lax.rem(space + k, nspace)},
                            device_id_type=pl.DeviceIdType.MESH)

    column = lax.rem(lax.broadcasted_iota(jnp.int32, (1, sites), 1), LZ)

    def roll(x, by):
        return pltpu.roll(x, by % sites, 1)

    def z_up(x):
        return jnp.where(column == LZ - 1, roll(x, LZ - 1), roll(x, -1))

    def z_down(x):
        return jnp.where(column == 0, roll(x, 1 - LZ), roll(x, 1))

    hops[0] = link_ref[0]
    hops[1] = back_ref[...]
    hops[2] = link_ref[1]
    hops[3] = roll(link_ref[1], LZ)
    hops[4] = link_ref[2]
    hops[5] = z_down(link_ref[2])

    pl.semaphore_wait(barrier, nvec - 1 + nspace - 1)

    def pass_on(slot, way):
        return pltpu.make_async_remote_copy(
            src_ref=gath.at[slot], dst_ref=gath.at[slot],
            send_sem=gsend.at[slot, way], recv_sem=grecv.at[slot],
            device_id={"vec": lax.rem(vec + (nvec - 1 if way else 1), nvec)},
            device_id_type=pl.DeviceIdType.MESH)

    def sends_up(source):
        return jnp.logical_and(source <= vec, vec < nvec - 1)

    def sends_down(source):
        return jnp.logical_and(source >= vec, vec > 0)

    def send_both(source, slot):
        @pl.when(sends_up(source))
        def _():
            pass_on(slot, 0).start()

        @pl.when(sends_down(source))
        def _():
            pass_on(slot, 1).start()

    def smear(c, carry):
        rows = pl.ds(pl.multiple_of(c * ROWS, ROWS), ROWS)

        def shift(comp, carry):
            x = v_ref[comp, rows, :].astype(jnp.float32)
            moved[0, comp] = plus_ref[comp, rows, :].astype(jnp.float32)
            moved[1, comp] = minus_ref[comp, rows, :].astype(jnp.float32)
            moved[2, comp] = roll(x, -LZ)
            moved[3, comp] = roll(x, LZ)
            moved[4, comp] = z_up(x)
            moved[5, comp] = z_down(x)
            return carry

        lax.fori_loop(0, 6, shift, 0)
        slot = vec * chunks + c

        def lanes(t, carry):
            at = pl.multiple_of(t * TILE, TILE)
            cols = pl.ds(at, TILE)
            re = [-6.0 * v_ref[2 * a, rows, cols].astype(jnp.float32) for a in range(3)]
            im = [-6.0 * v_ref[2 * a + 1, rows, cols].astype(jnp.float32) for a in range(3)]
            for h in range(6):
                for b in range(3):
                    vr = moved[h, 2 * b, :, cols]
                    vi = moved[h, 2 * b + 1, :, cols]
                    for a in range(3):
                        row = 3 * a + b if h % 2 == 0 else 3 * b + a
                        ur = hops[h, row : row + 1, cols]
                        ui = hops[h, 9 + row : 10 + row, cols]
                        if h % 2 == 0:
                            re[a] = re[a] + (ur * vr - ui * vi)
                            im[a] = im[a] + (ur * vi + ui * vr)
                        else:
                            re[a] = re[a] + (ur * vr + ui * vi)
                            im[a] = im[a] + (ur * vi - ui * vr)
            for a in range(3):
                base = 2 * a * sites
                gath[slot, :, pl.ds(pl.multiple_of(at + base, TILE), TILE)] = re[a].astype(jnp.bfloat16)
                gath[slot, :, pl.ds(pl.multiple_of(at + base + sites, TILE), TILE)] = im[a].astype(jnp.bfloat16)
            return carry

        lax.fori_loop(0, sites // TILE, lanes, 0)
        send_both(vec, slot)
        return carry

    lax.fori_loop(0, chunks, smear, 0)

    def reduce_copy(t, k):
        to = lax.rem(space + k, nspace)
        return pltpu.make_async_remote_copy(
            src_ref=outbox.at[t, to], dst_ref=inbox.at[t, k - 1],
            send_sem=rsend.at[t, k - 1], recv_sem=rrecv.at[t, k - 1],
            device_id={"space": to}, device_id_type=pl.DeviceIdType.MESH)

    def owner_slot(t):
        u = t - chunks
        inner = jnp.logical_and(vec > 0, vec < nvec - 1)
        toward = jnp.where(2 * vec < nvec, 1, -1)
        near = jnp.logical_and(inner, u < 2 * chunks)
        side = jnp.where(u % 2 == 0, toward, -toward)
        source = vec + jnp.where(
            near, side, toward * jnp.where(inner, u // chunks, u // chunks + 1)
        )
        c = jnp.where(near, u // 2, u % chunks)
        source = jnp.where(t < chunks, vec, source)
        c = jnp.where(t < chunks, t, c)
        return source, source * chunks + c

    block = momenta * ROWS

    def step(t, carry):
        source, slot = owner_slot(t)

        @pl.when(t >= chunks)
        def _():
            pass_on(slot, 0).wait_recv()
            send_both(source, slot)

        acc[...] = jnp.zeros_like(acc)
        parts = sites // PIECE

        def piece(q, carry):
            colour = q // parts
            tile = q % parts
            at = pl.multiple_of(tile * PIECE, PIECE)
            real_at = pl.multiple_of(colour * 2 * sites + tile * PIECE, PIECE)
            imag_at = pl.multiple_of(real_at + sites, PIECE)
            sr = gath[slot, :, pl.ds(real_at, PIECE)].astype(jnp.float32)
            si = gath[slot, :, pl.ds(imag_at, PIECE)].astype(jnp.float32)
            for p in range(momenta):
                cs = cos_ref[p : p + 1, pl.ds(at, PIECE)]
                sn = sin_ref[p : p + 1, pl.ds(at, PIECE)]
                both[p * ROWS : (p + 1) * ROWS, :] = (sr * cs + si * sn).astype(jnp.bfloat16)
                both[block + p * ROWS : block + (p + 1) * ROWS, :] = (si * cs - sr * sn).astype(jnp.bfloat16)
            dims = (((1,), (1,)), ((), ()))
            d1 = lax.dot_general(both[...], l_ref[:, pl.ds(real_at, PIECE)], dims,
                                 preferred_element_type=jnp.float32)
            d2 = lax.dot_general(both[...], l_ref[:, pl.ds(imag_at, PIECE)], dims,
                                 preferred_element_type=jnp.float32)
            acc[0] += d1[:block] + d2[block:]
            acc[1] += d1[block:] - d2[:block]
            return carry

        lax.fori_loop(0, 3 * parts, piece, 0)
        mine = share * ROWS
        for d in range(nspace):
            outbox[t, d] = acc[:, d * mine : (d + 1) * mine, :].astype(jnp.bfloat16)
        own[t] = acc[:, pl.ds(pl.multiple_of(space * mine, mine), mine), :]
        for m in range(1, nspace):
            reduce_copy(t, m).start()
        return carry

    lax.fori_loop(0, slots, step, 0)

    def finish(t, carry):
        source, slot = owner_slot(t)
        for m in range(1, nspace):
            reduce_copy(t, m).wait()
        value = own[t]
        for m in range(1, nspace):
            value = value + inbox[t, m - 1].astype(jnp.float32)
        at = pl.ds(pl.multiple_of(slot * ROWS, ROWS), ROWS)
        for r in range(2):
            for p in range(share):
                total[r, p, at, :] = value[r, p * ROWS : (p + 1) * ROWS, :]
        return carry

    lax.fori_loop(0, slots, finish, 0)
    scale = 1.0 / (8.0 * math.sqrt(3.0 * nspace * sites))
    hot = hot_ref[...]
    dims = (((0,), (0,)), ((), ()))
    for r in range(2):
        for p in range(share):
            x = total[r, p] * scale
            high = x.astype(jnp.bfloat16)
            low = (x - high.astype(jnp.float32)).astype(jnp.bfloat16)
            out_ref[p, r] = lax.dot_general(
                high, hot, dims, preferred_element_type=jnp.float32
            ) + lax.dot_general(low, hot, dims, preferred_element_type=jnp.float32)

    def drain(slot, carry):
        @pl.when(sends_up(slot // chunks))
        def _():
            pass_on(slot, 0).wait_send()

        @pl.when(sends_down(slot // chunks))
        def _():
            pass_on(slot, 1).wait_send()

        return carry

    lax.fori_loop(0, slots, drain, 0)


def local_fast(left_vecs, right_vecs, gauge_links, momenta, column_order):
    left = left_vecs.shape[0]
    right = right_vecs.shape[0]
    sites = left_vecs.shape[4]
    nspace = lax.axis_size("space")
    nvec = lax.axis_size("vec")
    count = momenta.shape[0]
    share = count // nspace
    chunks = right // ROWS
    slots = nvec * chunks
    center = right_vecs.transpose(2, 1, 3, 0, 4).reshape(6, right, sites)
    plus = from_behind(center, "space", -1)
    minus = from_behind(center, "space", 1)
    links = gauge_links.reshape(3, 18, sites)
    back = from_behind(links[0], "space", 1)
    rows = left_vecs.transpose(0, 2, 1, 3, 4).reshape(left, 6 * sites)
    cosine, sine = phase_tables(
        momenta, lax.axis_index("space")[None], nspace, sites // LZ, LZ, sites
    )
    cosine, sine = cosine.reshape(count, sites), sine.reshape(count, sites)
    hot = (jnp.arange(nvec * right)[:, None] == column_order[None]).astype(jnp.bfloat16)
    vmem = pl.BlockSpec(memory_space=pltpu.VMEM)
    mine = share * ROWS
    return pl.pallas_call(
        fast_kernel,
        out_shape=jax.ShapeDtypeStruct((share, 2, left, nvec * right), jnp.float32),
        in_specs=[vmem] * 9,
        out_specs=vmem,
        scratch_shapes=[
            pltpu.VMEM((6, 18, sites), jnp.float32),
            pltpu.VMEM((6, 6, ROWS, sites), jnp.float32),
            pltpu.VMEM((slots, ROWS, 6 * sites), jnp.bfloat16),
            pltpu.VMEM((2 * count * ROWS, PIECE), jnp.bfloat16),
            pltpu.VMEM((2, count * ROWS, left), jnp.float32),
            pltpu.VMEM((slots, nspace, 2, mine, left), jnp.bfloat16),
            pltpu.VMEM((slots, 2, mine, left), jnp.float32),
            pltpu.VMEM((slots, nspace - 1, 2, mine, left), jnp.bfloat16),
            pltpu.VMEM((2, share, nvec * right, left), jnp.float32),
            pltpu.SemaphoreType.DMA((slots, 2)),
            pltpu.SemaphoreType.DMA((slots,)),
            pltpu.SemaphoreType.DMA((slots, nspace - 1)),
            pltpu.SemaphoreType.DMA((slots, nspace - 1)),
        ],
        compiler_params=pltpu.CompilerParams(
            collective_id=0, has_side_effects=True, vmem_limit_bytes=56 * 1024 * 1024
        ),
        cost_estimate=pl.CostEstimate(flops=30_000_000_000, bytes_accessed=20_000_000, transcendentals=0),
    )(center, plus, minus, links, back, cosine, sine, hot, rows)


def local(left_vecs, right_vecs, gauge_links, momenta, column_order):
    nvec = lax.axis_size("vec")
    nspace = lax.axis_size("space")
    fits = (
        left_vecs.shape[3] == 1
        and right_vecs.shape[0] % ROWS == 0
        and nvec == 4
        and nspace == 4
        and left_vecs.shape[4] % PIECE == 0
        and momenta.shape[0] % nspace == 0
    )
    chosen = local_fast if fits else local_plain
    return chosen(left_vecs, right_vecs, gauge_links, momenta, column_order)


def solution(mesh):
    in_specs = (
        P("vec", "groups", None, "space", None),
        P("vec", "groups", None, "space", None),
        P("groups", None, None, None, "space", None),
        P(),
        P(),
    )
    out_specs = P("space", "groups", "vec", None)
    return jax.shard_map(local, mesh=mesh, in_specs=in_specs, out_specs=out_specs, check_vma=False)
```

```python
import math

import jax
import jax.numpy as jnp
from jax import lax
from jax.experimental import pallas as pl
from jax.experimental.pallas import tpu as pltpu
from jax.sharding import PartitionSpec as P

LZ = 48


def with_halo(block, sides, width):
    for axis, dim in sides:
        count = lax.axis_size(axis)
        forward = [(i, i + 1) for i in range(count - 1)]
        forward.append((count - 1, 0))
        backward = [(target, source) for source, target in forward]
        low = lax.ppermute(
            lax.slice_in_dim(block, block.shape[dim] - width, None, axis=dim), axis, forward
        )
        high = lax.ppermute(lax.slice_in_dim(block, 0, width, axis=dim), axis, backward)
        block = jnp.concatenate([low, block, high], axis=dim)
    return block


def from_behind(array, axis, by):
    length = lax.axis_size(axis)
    return lax.ppermute(array, axis, [(i, (i + by) % length) for i in range(length)])


def shifted(field, direction, step, width_z):
    length = field.shape[-1]
    if direction == 1:
        return jnp.roll(field, -step * width_z, axis=-1)
    column = jnp.arange(length) % width_z
    if step == 1:
        return jnp.where(
            column == width_z - 1,
            jnp.roll(field, width_z - 1, axis=-1),
            jnp.roll(field, -1, axis=-1),
        )
    return jnp.where(
        column == 0, jnp.roll(field, 1 - width_z, axis=-1), jnp.roll(field, 1, axis=-1)
    )


def color_mul(matrix, vectors):
    return jnp.sum(matrix[None] * vectors[:, None], axis=2)


def link_apply(link, vectors, adjoint):
    real_part = link[0]
    imag_part = link[1]
    if adjoint:
        real_part = jnp.swapaxes(real_part, 0, 1)
        imag_part = -jnp.swapaxes(imag_part, 0, 1)
    vec_real = vectors[:, 0]
    vec_imag = vectors[:, 1]
    out_real = color_mul(real_part, vec_real) - color_mul(imag_part, vec_imag)
    out_imag = color_mul(real_part, vec_imag) + color_mul(imag_part, vec_real)
    return jnp.stack([out_real, out_imag], axis=1)


def laplace_hops(center, plus_x, minus_x, links, back_x, width_z):
    total = link_apply(links[0], plus_x, False) + link_apply(back_x, minus_x, True)
    for direction in (1, 2):
        total = total + link_apply(links[direction], shifted(center, direction, 1, width_z), False)
        total = total + link_apply(
            shifted(links[direction], direction, -1, width_z),
            shifted(center, direction, -1, width_z),
            True,
        )
    return total - 6.0 * center


def phase_tables(momenta, global_x, count_x, width_y, width_z, length):
    sites = jnp.arange(length)
    coord_y = sites // width_z
    coord_z = sites % width_z
    two_pi = 2.0 * math.pi
    angle_x = jnp.mod(momenta[:, 0:1] * global_x[None], count_x).astype(jnp.float32) * (
        two_pi / count_x
    )
    angle_y = jnp.mod(momenta[:, 1:2] * coord_y[None], width_y).astype(jnp.float32) * (
        two_pi / width_y
    )
    angle_z = jnp.mod(momenta[:, 2:3] * coord_z[None], width_z).astype(jnp.float32) * (
        two_pi / width_z
    )
    angle = angle_x[:, :, None] + (angle_y + angle_z)[:, None, :]
    return (jnp.cos(angle), jnp.sin(angle))


def fold_phase(vectors, cosine, sine):
    values = vectors.astype(jnp.float32)
    vec_real = values[:, 0]
    vec_imag = values[:, 1]
    real_out = vec_real * cosine - vec_imag * sine
    imag_out = -(vec_real * sine + vec_imag * cosine)
    folded = jnp.stack([real_out, imag_out], axis=1).astype(jnp.bfloat16)
    return folded.reshape(folded.shape[0], 2, -1)


def combine_parts(product):
    return jnp.stack(
        [
            product[..., 0, :, 0] - product[..., 1, :, 1],
            product[..., 0, :, 1] + product[..., 1, :, 0],
        ],
        axis=-3,
    )


def contract(folded, stacked):
    product = lax.dot_general(
        folded, stacked, (((folded.ndim - 1,), (2,)), ((), ())), preferred_element_type=jnp.float32
    )
    return combine_parts(product)


def local_plain(left_vecs, right_vecs, gauge_links, momenta, column_order):
    local_x = left_vecs.shape[3]
    plane_size = left_vecs.shape[4]
    space_count = lax.axis_size("space")
    total_x = local_x * space_count
    padded = with_halo(right_vecs, (("space", 3),), 1)
    last_plane = gauge_links[0, :, :, :, local_x - 1 :, :]
    previous = from_behind(last_plane, "space", 1)
    back_x = jnp.concatenate([previous, gauge_links[0, :, :, :, : local_x - 1, :]], axis=3)
    global_x = lax.axis_index("space") * local_x + jnp.arange(local_x)
    cosine, sine = phase_tables(momenta, global_x, total_x, plane_size // LZ, LZ, plane_size)
    folded_all = jax.vmap(fold_phase, in_axes=(None, 0, 0))(left_vecs, cosine, sine)
    fields = padded.astype(jnp.float32)
    center = fields[:, :, :, 1:-1, :]
    smeared = laplace_hops(
        center, fields[:, :, :, 2:, :], fields[:, :, :, :-2, :], gauge_links, back_x, LZ
    ).astype(jnp.bfloat16)
    piece = lax.all_gather(smeared, "vec", axis=0, tiled=True)
    stacked = piece.reshape(piece.shape[0], 2, -1)
    mesons = contract(folded_all, stacked)
    hot = (jnp.arange(column_order.shape[0])[:, None] == column_order[None]).astype(jnp.float32)
    mesons = jnp.einsum("prij,jk->prik", mesons, hot, precision=lax.Precision.HIGHEST)
    scale = 1.0 / (8.0 * math.sqrt(3.0 * total_x * plane_size))
    share = lax.psum_scatter(mesons, "space", scatter_dimension=0, tiled=True)
    return share * scale


ROWS = 16
TILE = 256
PIECE = 768


def fast_kernel(
    v_ref, plus_ref, minus_ref, link_ref, back_ref, cos_ref, sin_ref, hot_ref, l_ref, out_ref,
    hops, moved, gath, both, acc, outbox, own, inbox, total,
    gsend, grecv, rsend, rrecv,
):
    nvec = lax.axis_size("vec")
    nspace = lax.axis_size("space")
    vec = lax.axis_index("vec")
    space = lax.axis_index("space")
    sites = v_ref.shape[2]
    chunks = v_ref.shape[1] // ROWS
    momenta = cos_ref.shape[0]
    share = momenta // nspace
    slots = nvec * chunks
    left = l_ref.shape[0]

    barrier = pltpu.get_barrier_semaphore()
    for k in range(1, nvec):
        pl.semaphore_signal(barrier, inc=1, device_id={"vec": lax.rem(vec + k, nvec)},
                            device_id_type=pl.DeviceIdType.MESH)
    for k in range(1, nspace):
        pl.semaphore_signal(barrier, inc=1, device_id={"space": lax.rem(space + k, nspace)},
                            device_id_type=pl.DeviceIdType.MESH)

    column = lax.rem(lax.broadcasted_iota(jnp.int32, (1, sites), 1), LZ)

    def roll(x, by):
        return pltpu.roll(x, by % sites, 1)

    def z_up(x):
        return jnp.where(column == LZ - 1, roll(x, LZ - 1), roll(x, -1))

    def z_down(x):
        return jnp.where(column == 0, roll(x, 1 - LZ), roll(x, 1))

    for row in range(18):
        hops[1, row : row + 1, :] = back_ref[row]
        for d in range(3):
            hops[2 * d, row : row + 1, :] = link_ref[18 * d + row]
    hops[3] = roll(hops[2], LZ)
    hops[5] = z_down(hops[4])

    pl.semaphore_wait(barrier, nvec - 1 + nspace - 1)

    parts = sites // PIECE

    def pass_on(slot, part, way):
        return pltpu.make_async_remote_copy(
            src_ref=gath.at[slot, part], dst_ref=gath.at[slot, part],
            send_sem=gsend.at[slot, part, way], recv_sem=grecv.at[slot, part],
            device_id={"vec": lax.rem(vec + (nvec - 1 if way else 1), nvec)},
            device_id_type=pl.DeviceIdType.MESH)

    def sends_up(source):
        return jnp.logical_and(source <= vec, vec < nvec - 1)

    def sends_down(source):
        return jnp.logical_and(source >= vec, vec > 0)

    def send_both(source, slot, part):
        @pl.when(sends_up(source))
        def _():
            pass_on(slot, part, 0).start()

        @pl.when(sends_down(source))
        def _():
            pass_on(slot, part, 1).start()

    def smear(c, carry):
        rows = pl.ds(pl.multiple_of(c * ROWS, ROWS), ROWS)

        def shift(comp, carry):
            x = v_ref[comp, rows, :].astype(jnp.float32)
            moved[0, comp] = plus_ref[comp, rows, :].astype(jnp.float32)
            moved[1, comp] = minus_ref[comp, rows, :].astype(jnp.float32)
            moved[2, comp] = roll(x, -LZ)
            moved[3, comp] = roll(x, LZ)
            moved[4, comp] = z_up(x)
            moved[5, comp] = z_down(x)
            return carry

        lax.fori_loop(0, 6, shift, 0)
        slot = vec * chunks + c

        def lanes(t, carry):
            at = pl.multiple_of(t * TILE, TILE)
            cols = pl.ds(at, TILE)
            re = [-6.0 * v_ref[2 * a, rows, cols].astype(jnp.float32) for a in range(3)]
            im = [-6.0 * v_ref[2 * a + 1, rows, cols].astype(jnp.float32) for a in range(3)]
            for h in range(6):
                for b in range(3):
                    vr = moved[h, 2 * b, :, cols]
                    vi = moved[h, 2 * b + 1, :, cols]
                    for a in range(3):
                        row = 3 * a + b if h % 2 == 0 else 3 * b + a
                        ur = hops[h, row : row + 1, cols]
                        ui = hops[h, 9 + row : 10 + row, cols]
                        if h % 2 == 0:
                            re[a] = re[a] + (ur * vr - ui * vi)
                            im[a] = im[a] + (ur * vi + ui * vr)
                        else:
                            re[a] = re[a] + (ur * vr + ui * vi)
                            im[a] = im[a] + (ur * vi - ui * vr)
            for a in range(3):
                part = t // (PIECE // TILE)
                inside = pl.ds(pl.multiple_of((t % (PIECE // TILE)) * TILE, TILE), TILE)
                gath[slot, part, 2 * a, :, inside] = re[a].astype(jnp.bfloat16)
                gath[slot, part, 2 * a + 1, :, inside] = im[a].astype(jnp.bfloat16)
            return carry

        def one_part(part, carry):
            lax.fori_loop(part * (PIECE // TILE), (part + 1) * (PIECE // TILE), lanes, 0)
            send_both(vec, slot, part)
            return carry

        lax.fori_loop(0, parts, one_part, 0)
        return carry

    lax.fori_loop(0, chunks, smear, 0)

    def reduce_copy(t, k):
        to = lax.rem(space + k, nspace)
        return pltpu.make_async_remote_copy(
            src_ref=outbox.at[t, to], dst_ref=inbox.at[t, k - 1],
            send_sem=rsend.at[t, k - 1], recv_sem=rrecv.at[t, k - 1],
            device_id={"space": to}, device_id_type=pl.DeviceIdType.MESH)

    def owner_slot(t):
        u = t - chunks
        inner = jnp.logical_and(vec > 0, vec < nvec - 1)
        toward = jnp.where(2 * vec < nvec, 1, -1)
        near = jnp.logical_and(inner, u < 2 * chunks)
        side = jnp.where(u % 2 == 0, toward, -toward)
        source = vec + jnp.where(
            near, side, toward * jnp.where(inner, u // chunks, u // chunks + 1)
        )
        c = jnp.where(near, u // 2, u % chunks)
        source = jnp.where(t < chunks, vec, source)
        c = jnp.where(t < chunks, t, c)
        return source, source * chunks + c

    block = momenta * ROWS

    def step(t, carry):
        source, slot = owner_slot(t)

        acc[...] = jnp.zeros_like(acc)

        def piece(q, carry):
            colour = q % 3
            tile = q // 3

            @pl.when(jnp.logical_and(t >= chunks, colour == 0))
            def _():
                pass_on(slot, tile, 0).wait_recv()
                send_both(source, slot, tile)

            at = pl.multiple_of(tile * PIECE, PIECE)
            real_at = pl.multiple_of(colour * 2 * sites + tile * PIECE, PIECE)
            imag_at = pl.multiple_of(real_at + sites, PIECE)
            sr = gath[slot, tile, 2 * colour].astype(jnp.float32)
            si = gath[slot, tile, 2 * colour + 1].astype(jnp.float32)
            for p in range(momenta):
                cs = cos_ref[p : p + 1, pl.ds(at, PIECE)]
                sn = sin_ref[p : p + 1, pl.ds(at, PIECE)]
                both[p * ROWS : (p + 1) * ROWS, :] = (sr * cs + si * sn).astype(jnp.bfloat16)
                both[block + p * ROWS : block + (p + 1) * ROWS, :] = (si * cs - sr * sn).astype(jnp.bfloat16)
            dims = (((1,), (1,)), ((), ()))
            d1 = lax.dot_general(both[...], l_ref[:, pl.ds(real_at, PIECE)], dims,
                                 preferred_element_type=jnp.float32)
            d2 = lax.dot_general(both[...], l_ref[:, pl.ds(imag_at, PIECE)], dims,
                                 preferred_element_type=jnp.float32)
            acc[0] += d1[:block] + d2[block:]
            acc[1] += d1[block:] - d2[:block]
            return carry

        lax.fori_loop(0, 3 * parts, piece, 0)
        mine = share * ROWS
        for d in range(nspace):
            outbox[t, d] = acc[:, d * mine : (d + 1) * mine, :].astype(jnp.bfloat16)
        own[t] = acc[:, pl.ds(pl.multiple_of(space * mine, mine), mine), :]
        for m in range(1, nspace):
            reduce_copy(t, m).start()

        @pl.when(t >= 2)
        def _():
            finish(t - 2)

        return carry

    def finish(t):
        source, slot = owner_slot(t)
        for m in range(1, nspace):
            reduce_copy(t, m).wait()
        value = own[t]
        for m in range(1, nspace):
            value = value + inbox[t, m - 1].astype(jnp.float32)
        at = pl.ds(pl.multiple_of(slot * ROWS, ROWS), ROWS)
        for r in range(2):
            for p in range(share):
                total[r, p, at, :] = value[r, p * ROWS : (p + 1) * ROWS, :]

    lax.fori_loop(0, slots, step, 0)
    finish(slots - 2)
    finish(slots - 1)
    scale = 1.0 / (8.0 * math.sqrt(3.0 * nspace * sites))
    hot = hot_ref[...]
    dims = (((0,), (0,)), ((), ()))
    for r in range(2):
        for p in range(share):
            x = total[r, p] * scale
            high = x.astype(jnp.bfloat16)
            low = (x - high.astype(jnp.float32)).astype(jnp.bfloat16)
            out_ref[p, r] = lax.dot_general(
                high, hot, dims, preferred_element_type=jnp.float32
            ) + lax.dot_general(low, hot, dims, preferred_element_type=jnp.float32)

    def drain(n, carry):
        slot = n // parts
        part = n % parts

        @pl.when(sends_up(slot // chunks))
        def _():
            pass_on(slot, part, 0).wait_send()

        @pl.when(sends_down(slot // chunks))
        def _():
            pass_on(slot, part, 1).wait_send()

        return carry

    lax.fori_loop(0, slots * parts, drain, 0)


def local_fast(left_vecs, right_vecs, gauge_links, momenta, column_order):
    left = left_vecs.shape[0]
    right = right_vecs.shape[0]
    sites = left_vecs.shape[4]
    nspace = lax.axis_size("space")
    nvec = lax.axis_size("vec")
    count = momenta.shape[0]
    share = count // nspace
    chunks = right // ROWS
    slots = nvec * chunks
    center = right_vecs.transpose(2, 1, 3, 0, 4).reshape(6, right, sites)
    plus = from_behind(center, "space", -1)
    minus = from_behind(center, "space", 1)
    links = gauge_links.reshape(54, 1, sites)
    back = from_behind(links[:18], "space", 1)
    rows = left_vecs.transpose(0, 2, 1, 3, 4).reshape(left, 6 * sites)
    cosine, sine = phase_tables(
        momenta, lax.axis_index("space")[None], nspace, sites // LZ, LZ, sites
    )
    cosine, sine = cosine.reshape(count, sites), sine.reshape(count, sites)
    hot = (jnp.arange(nvec * right)[:, None] == column_order[None]).astype(jnp.bfloat16)
    vmem = pl.BlockSpec(memory_space=pltpu.VMEM)
    mine = share * ROWS
    return pl.pallas_call(
        fast_kernel,
        out_shape=jax.ShapeDtypeStruct((share, 2, left, nvec * right), jnp.float32),
        in_specs=[vmem] * 9,
        out_specs=vmem,
        scratch_shapes=[
            pltpu.VMEM((6, 18, sites), jnp.float32),
            pltpu.VMEM((6, 6, ROWS, sites), jnp.float32),
            pltpu.VMEM((slots, sites // PIECE, 6, ROWS, PIECE), jnp.bfloat16),
            pltpu.VMEM((2 * count * ROWS, PIECE), jnp.bfloat16),
            pltpu.VMEM((2, count * ROWS, left), jnp.float32),
            pltpu.VMEM((slots, nspace, 2, mine, left), jnp.bfloat16),
            pltpu.VMEM((slots, 2, mine, left), jnp.float32),
            pltpu.VMEM((slots, nspace - 1, 2, mine, left), jnp.bfloat16),
            pltpu.VMEM((2, share, nvec * right, left), jnp.float32),
            pltpu.SemaphoreType.DMA((slots, sites // PIECE, 2)),
            pltpu.SemaphoreType.DMA((slots, sites // PIECE)),
            pltpu.SemaphoreType.DMA((slots, nspace - 1)),
            pltpu.SemaphoreType.DMA((slots, nspace - 1)),
        ],
        compiler_params=pltpu.CompilerParams(
            collective_id=0, has_side_effects=True, vmem_limit_bytes=56 * 1024 * 1024
        ),
        cost_estimate=pl.CostEstimate(flops=30_000_000_000, bytes_accessed=20_000_000, transcendentals=0),
    )(center, plus, minus, links, back, cosine, sine, hot, rows)


def local(left_vecs, right_vecs, gauge_links, momenta, column_order):
    nvec = lax.axis_size("vec")
    nspace = lax.axis_size("space")
    fits = (
        left_vecs.shape[3] == 1
        and right_vecs.shape[0] % ROWS == 0
        and nvec == 4
        and nspace == 4
        and left_vecs.shape[4] % PIECE == 0
        and momenta.shape[0] % nspace == 0
    )
    chosen = local_fast if fits else local_plain
    return chosen(left_vecs, right_vecs, gauge_links, momenta, column_order)


def solution(mesh):
    in_specs = (
        P("vec", "groups", None, "space", None),
        P("vec", "groups", None, "space", None),
        P("groups", None, None, None, "space", None),
        P(),
        P(),
    )
    out_specs = P("space", "groups", "vec", None)
    return jax.shard_map(local, mesh=mesh, in_specs=in_specs, out_specs=out_specs, check_vma=False)
```

```python
import math

import jax
import jax.numpy as jnp
from jax import lax
from jax.experimental import pallas as pl
from jax.experimental.pallas import tpu as pltpu
from jax.sharding import PartitionSpec as P

LZ = 48


def with_halo(block, sides, width):
    for axis, dim in sides:
        count = lax.axis_size(axis)
        forward = [(i, i + 1) for i in range(count - 1)]
        forward.append((count - 1, 0))
        backward = [(target, source) for source, target in forward]
        low = lax.ppermute(
            lax.slice_in_dim(block, block.shape[dim] - width, None, axis=dim), axis, forward
        )
        high = lax.ppermute(lax.slice_in_dim(block, 0, width, axis=dim), axis, backward)
        block = jnp.concatenate([low, block, high], axis=dim)
    return block


def from_behind(array, axis, by):
    length = lax.axis_size(axis)
    return lax.ppermute(array, axis, [(i, (i + by) % length) for i in range(length)])


def shifted(field, direction, step, width_z):
    length = field.shape[-1]
    if direction == 1:
        return jnp.roll(field, -step * width_z, axis=-1)
    column = jnp.arange(length) % width_z
    if step == 1:
        return jnp.where(
            column == width_z - 1,
            jnp.roll(field, width_z - 1, axis=-1),
            jnp.roll(field, -1, axis=-1),
        )
    return jnp.where(
        column == 0, jnp.roll(field, 1 - width_z, axis=-1), jnp.roll(field, 1, axis=-1)
    )


def color_mul(matrix, vectors):
    return jnp.sum(matrix[None] * vectors[:, None], axis=2)


def link_apply(link, vectors, adjoint):
    real_part = link[0]
    imag_part = link[1]
    if adjoint:
        real_part = jnp.swapaxes(real_part, 0, 1)
        imag_part = -jnp.swapaxes(imag_part, 0, 1)
    vec_real = vectors[:, 0]
    vec_imag = vectors[:, 1]
    out_real = color_mul(real_part, vec_real) - color_mul(imag_part, vec_imag)
    out_imag = color_mul(real_part, vec_imag) + color_mul(imag_part, vec_real)
    return jnp.stack([out_real, out_imag], axis=1)


def laplace_hops(center, plus_x, minus_x, links, back_x, width_z):
    total = link_apply(links[0], plus_x, False) + link_apply(back_x, minus_x, True)
    for direction in (1, 2):
        total = total + link_apply(links[direction], shifted(center, direction, 1, width_z), False)
        total = total + link_apply(
            shifted(links[direction], direction, -1, width_z),
            shifted(center, direction, -1, width_z),
            True,
        )
    return total - 6.0 * center


def phase_tables(momenta, global_x, count_x, width_y, width_z, length):
    sites = jnp.arange(length)
    coord_y = sites // width_z
    coord_z = sites % width_z
    two_pi = 2.0 * math.pi
    angle_x = jnp.mod(momenta[:, 0:1] * global_x[None], count_x).astype(jnp.float32) * (
        two_pi / count_x
    )
    angle_y = jnp.mod(momenta[:, 1:2] * coord_y[None], width_y).astype(jnp.float32) * (
        two_pi / width_y
    )
    angle_z = jnp.mod(momenta[:, 2:3] * coord_z[None], width_z).astype(jnp.float32) * (
        two_pi / width_z
    )
    angle = angle_x[:, :, None] + (angle_y + angle_z)[:, None, :]
    return (jnp.cos(angle), jnp.sin(angle))


def fold_phase(vectors, cosine, sine):
    values = vectors.astype(jnp.float32)
    vec_real = values[:, 0]
    vec_imag = values[:, 1]
    real_out = vec_real * cosine - vec_imag * sine
    imag_out = -(vec_real * sine + vec_imag * cosine)
    folded = jnp.stack([real_out, imag_out], axis=1).astype(jnp.bfloat16)
    return folded.reshape(folded.shape[0], 2, -1)


def combine_parts(product):
    return jnp.stack(
        [
            product[..., 0, :, 0] - product[..., 1, :, 1],
            product[..., 0, :, 1] + product[..., 1, :, 0],
        ],
        axis=-3,
    )


def contract(folded, stacked):
    product = lax.dot_general(
        folded, stacked, (((folded.ndim - 1,), (2,)), ((), ())), preferred_element_type=jnp.float32
    )
    return combine_parts(product)


def local_plain(left_vecs, right_vecs, gauge_links, momenta, column_order):
    local_x = left_vecs.shape[3]
    plane_size = left_vecs.shape[4]
    space_count = lax.axis_size("space")
    total_x = local_x * space_count
    padded = with_halo(right_vecs, (("space", 3),), 1)
    last_plane = gauge_links[0, :, :, :, local_x - 1 :, :]
    previous = from_behind(last_plane, "space", 1)
    back_x = jnp.concatenate([previous, gauge_links[0, :, :, :, : local_x - 1, :]], axis=3)
    global_x = lax.axis_index("space") * local_x + jnp.arange(local_x)
    cosine, sine = phase_tables(momenta, global_x, total_x, plane_size // LZ, LZ, plane_size)
    folded_all = jax.vmap(fold_phase, in_axes=(None, 0, 0))(left_vecs, cosine, sine)
    fields = padded.astype(jnp.float32)
    center = fields[:, :, :, 1:-1, :]
    smeared = laplace_hops(
        center, fields[:, :, :, 2:, :], fields[:, :, :, :-2, :], gauge_links, back_x, LZ
    ).astype(jnp.bfloat16)
    piece = lax.all_gather(smeared, "vec", axis=0, tiled=True)
    stacked = piece.reshape(piece.shape[0], 2, -1)
    mesons = contract(folded_all, stacked)
    hot = (jnp.arange(column_order.shape[0])[:, None] == column_order[None]).astype(jnp.float32)
    mesons = jnp.einsum("prij,jk->prik", mesons, hot, precision=lax.Precision.HIGHEST)
    scale = 1.0 / (8.0 * math.sqrt(3.0 * total_x * plane_size))
    share = lax.psum_scatter(mesons, "space", scatter_dimension=0, tiled=True)
    return share * scale


ROWS = 16
TILE = 256
PIECE = 768


def fast_kernel(
    v_ref, plus_ref, minus_ref, link_ref, back_ref, cos_ref, sin_ref, l_ref, total,
    hops, moved, gath, both, acc, outbox, own, inbox,
    gsend, grecv, rsend, rrecv,
):
    nvec = lax.axis_size("vec")
    nspace = lax.axis_size("space")
    vec = lax.axis_index("vec")
    space = lax.axis_index("space")
    sites = v_ref.shape[2]
    chunks = v_ref.shape[1] // ROWS
    momenta = cos_ref.shape[0]
    share = momenta // nspace
    slots = nvec * chunks
    left = l_ref.shape[0]

    barrier = pltpu.get_barrier_semaphore()
    for k in range(1, nvec):
        pl.semaphore_signal(barrier, inc=1, device_id={"vec": lax.rem(vec + k, nvec)},
                            device_id_type=pl.DeviceIdType.MESH)
    for k in range(1, nspace):
        pl.semaphore_signal(barrier, inc=1, device_id={"space": lax.rem(space + k, nspace)},
                            device_id_type=pl.DeviceIdType.MESH)

    column = lax.rem(lax.broadcasted_iota(jnp.int32, (1, sites), 1), LZ)

    def roll(x, by):
        return pltpu.roll(x, by % sites, 1)

    def z_up(x):
        return jnp.where(column == LZ - 1, roll(x, LZ - 1), roll(x, -1))

    def z_down(x):
        return jnp.where(column == 0, roll(x, 1 - LZ), roll(x, 1))

    for row in range(18):
        hops[1, row : row + 1, :] = back_ref[row]
        for d in range(3):
            hops[2 * d, row : row + 1, :] = link_ref[18 * d + row]
    hops[3] = roll(hops[2], LZ)
    hops[5] = z_down(hops[4])

    pl.semaphore_wait(barrier, nvec - 1 + nspace - 1)

    parts = sites // PIECE

    def pass_on(slot, part, way):
        return pltpu.make_async_remote_copy(
            src_ref=gath.at[slot, part], dst_ref=gath.at[slot, part],
            send_sem=gsend.at[slot, part, way], recv_sem=grecv.at[slot, part],
            device_id={"vec": lax.rem(vec + (nvec - 1 if way else 1), nvec)},
            device_id_type=pl.DeviceIdType.MESH)

    def sends_up(source):
        return jnp.logical_and(source <= vec, vec < nvec - 1)

    def sends_down(source):
        return jnp.logical_and(source >= vec, vec > 0)

    def send_both(source, slot, part):
        @pl.when(sends_up(source))
        def _():
            pass_on(slot, part, 0).start()

        @pl.when(sends_down(source))
        def _():
            pass_on(slot, part, 1).start()

    def smear(c, carry):
        rows = pl.ds(pl.multiple_of(c * ROWS, ROWS), ROWS)

        def shift(comp, carry):
            x = v_ref[comp, rows, :].astype(jnp.float32)
            moved[0, comp] = roll(x, -LZ)
            moved[1, comp] = roll(x, LZ)
            moved[2, comp] = z_up(x)
            moved[3, comp] = z_down(x)
            return carry

        lax.fori_loop(0, 6, shift, 0)
        slot = vec * chunks + c

        def lanes(t, carry):
            at = pl.multiple_of(t * TILE, TILE)
            cols = pl.ds(at, TILE)
            re = [-6.0 * v_ref[2 * a, rows, cols].astype(jnp.float32) for a in range(3)]
            im = [-6.0 * v_ref[2 * a + 1, rows, cols].astype(jnp.float32) for a in range(3)]
            for h in range(6):
                for b in range(3):
                    if h < 2:
                        halo = minus_ref if h else plus_ref
                        vr = halo[2 * b, rows, cols].astype(jnp.float32)
                        vi = halo[2 * b + 1, rows, cols].astype(jnp.float32)
                    else:
                        vr = moved[h - 2, 2 * b, :, cols]
                        vi = moved[h - 2, 2 * b + 1, :, cols]
                    for a in range(3):
                        row = 3 * a + b if h % 2 == 0 else 3 * b + a
                        ur = hops[h, row : row + 1, cols]
                        ui = hops[h, 9 + row : 10 + row, cols]
                        if h % 2 == 0:
                            re[a] = re[a] + (ur * vr - ui * vi)
                            im[a] = im[a] + (ur * vi + ui * vr)
                        else:
                            re[a] = re[a] + (ur * vr + ui * vi)
                            im[a] = im[a] + (ur * vi - ui * vr)
            for a in range(3):
                part = t // (PIECE // TILE)
                inside = pl.ds(pl.multiple_of((t % (PIECE // TILE)) * TILE, TILE), TILE)
                gath[slot, part, 2 * a, :, inside] = re[a].astype(jnp.bfloat16)
                gath[slot, part, 2 * a + 1, :, inside] = im[a].astype(jnp.bfloat16)
            return carry

        def one_part(part, carry):
            lax.fori_loop(part * (PIECE // TILE), (part + 1) * (PIECE // TILE), lanes, 0)
            send_both(vec, slot, part)
            return carry

        lax.fori_loop(0, parts, one_part, 0)
        return carry

    lax.fori_loop(0, chunks, smear, 0)

    def reduce_copy(t, k):
        to = lax.rem(space + k, nspace)
        return pltpu.make_async_remote_copy(
            src_ref=outbox.at[t, to], dst_ref=inbox.at[t, k - 1],
            send_sem=rsend.at[t, k - 1], recv_sem=rrecv.at[t, k - 1],
            device_id={"space": to}, device_id_type=pl.DeviceIdType.MESH)

    def owner_slot(t):
        u = t - chunks
        inner = jnp.logical_and(vec > 0, vec < nvec - 1)
        toward = jnp.where(2 * vec < nvec, 1, -1)
        near = jnp.logical_and(inner, u < 2 * chunks)
        side = jnp.where(u % 2 == 0, toward, -toward)
        source = vec + jnp.where(
            near, side, toward * jnp.where(inner, u // chunks, u // chunks + 1)
        )
        c = jnp.where(near, u // 2, u % chunks)
        source = jnp.where(t < chunks, vec, source)
        c = jnp.where(t < chunks, t, c)
        return source, source * chunks + c

    block = momenta * ROWS

    def step(t, carry):
        source, slot = owner_slot(t)

        acc[...] = jnp.zeros_like(acc)

        def piece(q, carry):
            colour = q % 3
            tile = q // 3

            @pl.when(jnp.logical_and(t >= chunks, colour == 0))
            def _():
                pass_on(slot, tile, 0).wait_recv()
                send_both(source, slot, tile)

            at = pl.multiple_of(tile * PIECE, PIECE)
            real_at = pl.multiple_of(colour * 2 * sites + tile * PIECE, PIECE)
            imag_at = pl.multiple_of(real_at + sites, PIECE)
            sr = gath[slot, tile, 2 * colour].astype(jnp.float32)
            si = gath[slot, tile, 2 * colour + 1].astype(jnp.float32)
            for p in range(momenta):
                cs = cos_ref[p : p + 1, pl.ds(at, PIECE)]
                sn = sin_ref[p : p + 1, pl.ds(at, PIECE)]
                both[p * ROWS : (p + 1) * ROWS, :] = (sr * cs + si * sn).astype(jnp.bfloat16)
                both[block + p * ROWS : block + (p + 1) * ROWS, :] = (si * cs - sr * sn).astype(jnp.bfloat16)
            dims = (((1,), (1,)), ((), ()))
            d1 = lax.dot_general(both[...], l_ref[:, pl.ds(real_at, PIECE)], dims,
                                 preferred_element_type=jnp.float32)
            d2 = lax.dot_general(both[...], l_ref[:, pl.ds(imag_at, PIECE)], dims,
                                 preferred_element_type=jnp.float32)
            acc[0] += d1[:block] + d2[block:]
            acc[1] += d1[block:] - d2[:block]
            return carry

        lax.fori_loop(0, 3 * parts, piece, 0)
        mine = share * ROWS
        for d in range(nspace):
            outbox[t, d] = acc[:, d * mine : (d + 1) * mine, :].astype(jnp.bfloat16)
        own[t] = acc[:, pl.ds(pl.multiple_of(space * mine, mine), mine), :]
        for m in range(1, nspace):
            reduce_copy(t, m).start()

        @pl.when(t >= 2)
        def _():
            finish(t - 2)

        return carry

    def finish(t):
        source, slot = owner_slot(t)
        for m in range(1, nspace):
            reduce_copy(t, m).wait()
        value = own[t]
        for m in range(1, nspace):
            value = value + inbox[t, m - 1].astype(jnp.float32)
        at = pl.ds(pl.multiple_of(slot * ROWS, ROWS), ROWS)
        for r in range(2):
            for p in range(share):
                total[r, p, at, :] = value[r, p * ROWS : (p + 1) * ROWS, :]

    lax.fori_loop(0, slots, step, 0)
    finish(slots - 2)
    finish(slots - 1)

    def drain(n, carry):
        slot = n // parts
        part = n % parts

        @pl.when(sends_up(slot // chunks))
        def _():
            pass_on(slot, part, 0).wait_send()

        @pl.when(sends_down(slot // chunks))
        def _():
            pass_on(slot, part, 1).wait_send()

        return carry

    lax.fori_loop(0, slots * parts, drain, 0)


def turn_kernel(scale, total_ref, hot_ref, out_ref):
    hot = hot_ref[...]
    dims = (((0,), (0,)), ((), ()))
    for r in range(2):
        for p in range(out_ref.shape[0]):
            x = total_ref[r, p] * scale
            high = x.astype(jnp.bfloat16)
            low = (x - high.astype(jnp.float32)).astype(jnp.bfloat16)
            out_ref[p, r] = lax.dot_general(
                high, hot, dims, preferred_element_type=jnp.float32
            ) + lax.dot_general(low, hot, dims, preferred_element_type=jnp.float32)


def local_fast(left_vecs, right_vecs, gauge_links, momenta, column_order):
    left = left_vecs.shape[0]
    right = right_vecs.shape[0]
    sites = left_vecs.shape[4]
    nspace = lax.axis_size("space")
    nvec = lax.axis_size("vec")
    count = momenta.shape[0]
    share = count // nspace
    chunks = right // ROWS
    slots = nvec * chunks
    center = right_vecs.transpose(2, 1, 3, 0, 4).reshape(6, right, sites)
    plus = from_behind(center, "space", -1)
    minus = from_behind(center, "space", 1)
    links = gauge_links.reshape(54, 1, sites)
    back = from_behind(links[:18], "space", 1)
    rows = left_vecs.transpose(0, 2, 1, 3, 4).reshape(left, 6 * sites)
    cosine, sine = phase_tables(
        momenta, lax.axis_index("space")[None], nspace, sites // LZ, LZ, sites
    )
    cosine, sine = cosine.reshape(count, sites), sine.reshape(count, sites)
    hot = (jnp.arange(nvec * right)[:, None] == column_order[None]).astype(jnp.bfloat16)
    vmem = pl.BlockSpec(memory_space=pltpu.VMEM)
    mine = share * ROWS
    total = pl.pallas_call(
        fast_kernel,
        out_shape=jax.ShapeDtypeStruct((2, share, nvec * right, left), jnp.float32),
        in_specs=[vmem] * 8,
        out_specs=vmem,
        scratch_shapes=[
            pltpu.VMEM((6, 18, sites), jnp.float32),
            pltpu.VMEM((4, 6, ROWS, sites), jnp.float32),
            pltpu.VMEM((slots, sites // PIECE, 6, ROWS, PIECE), jnp.bfloat16),
            pltpu.VMEM((2 * count * ROWS, PIECE), jnp.bfloat16),
            pltpu.VMEM((2, count * ROWS, left), jnp.float32),
            pltpu.VMEM((slots, nspace, 2, mine, left), jnp.bfloat16),
            pltpu.VMEM((slots, 2, mine, left), jnp.float32),
            pltpu.VMEM((slots, nspace - 1, 2, mine, left), jnp.bfloat16),
            pltpu.SemaphoreType.DMA((slots, sites // PIECE, 2)),
            pltpu.SemaphoreType.DMA((slots, sites // PIECE)),
            pltpu.SemaphoreType.DMA((slots, nspace - 1)),
            pltpu.SemaphoreType.DMA((slots, nspace - 1)),
        ],
        compiler_params=pltpu.CompilerParams(
            collective_id=0, has_side_effects=True, vmem_limit_bytes=56 * 1024 * 1024
        ),
        cost_estimate=pl.CostEstimate(flops=30_000_000_000, bytes_accessed=20_000_000, transcendentals=0),
    )(center, plus, minus, links, back, cosine, sine, rows)
    scale = 1.0 / (8.0 * math.sqrt(3.0 * nspace * sites))
    return pl.pallas_call(
        lambda *refs: turn_kernel(scale, *refs),
        out_shape=jax.ShapeDtypeStruct((share, 2, left, nvec * right), jnp.float32),
        in_specs=[vmem] * 2,
        out_specs=vmem,
        compiler_params=pltpu.CompilerParams(vmem_limit_bytes=16 * 1024 * 1024),
    )(total, hot)


def local(left_vecs, right_vecs, gauge_links, momenta, column_order):
    nvec = lax.axis_size("vec")
    nspace = lax.axis_size("space")
    fits = (
        left_vecs.shape[3] == 1
        and right_vecs.shape[0] % ROWS == 0
        and nvec == 4
        and nspace == 4
        and left_vecs.shape[4] % PIECE == 0
        and momenta.shape[0] % nspace == 0
    )
    chosen = local_fast if fits else local_plain
    return chosen(left_vecs, right_vecs, gauge_links, momenta, column_order)


def solution(mesh):
    in_specs = (
        P("vec", "groups", None, "space", None),
        P("vec", "groups", None, "space", None),
        P("groups", None, None, None, "space", None),
        P(),
        P(),
    )
    out_specs = P("space", "groups", "vec", None)
    return jax.shard_map(local, mesh=mesh, in_specs=in_specs, out_specs=out_specs, check_vma=False)
```
